128 devices in a mesh: seq: 16 (over y, x_hi, core), dp: 8 (over x_lo, z).
Axes of the slice: x: 4 (x_hi: 2, x_lo: 2; x = x_hi * 2 + x_lo), y: 4, z: 4, core: 2. Of those that a mesh axis runs over, the one named last changes fastest.
Arguments:
- query: bfloat16 [8, 2048, 2048], P('dp', 'seq'), may hold values from -6 to 6
- key: bfloat16 [8, 2048, 2048], P('dp', 'seq'), may hold values from -6 to 6
- value: bfloat16 [8, 2048, 4096], P('dp', 'seq'), may hold values from -6 to 6
- gate_in: bfloat16 [8, 2048, 4096], P('dp', 'seq'), may hold values from -6 to 6
- decay_in: bfloat16 [8, 2048, 32], P('dp', 'seq'), may hold values from -6 to 6
- beta_in: bfloat16 [8, 2048, 32], P('dp', 'seq'), may hold values from -6 to 6
- a_log: float32 [32], replicated, may hold values from -10 to -3
- dt_bias: float32 [32], replicated, may hold values from -2 to 1
- norm_weight: float32 [128], replicated, may hold values from 0.1 to 1.9
- d_out: bfloat16 [8, 2048, 4096], P('dp', 'seq'), may hold values from -6 to 6
Outputs:
- mixed: bfloat16 [8, 2048, 4096], P('dp', 'seq')
- d_query: bfloat16 [8, 2048, 2048], P('dp', 'seq')
- d_key: bfloat16 [8, 2048, 2048], P('dp', 'seq')
- d_value: bfloat16 [8, 2048, 4096], P('dp', 'seq')
- d_gate: bfloat16 [8, 2048, 4096], P('dp', 'seq')
- d_decay: bfloat16 [8, 2048, 32], P('dp', 'seq')
- d_beta: bfloat16 [8, 2048, 32], P('dp', 'seq')
- d_a_log: float32 [32], P('seq')
- d_dt_bias: float32 [32], P('seq')
- d_norm_weight: float32 [128], replicated
The draws below stay inside these ranges and needn't reach their ends.
All inputs are finite; a program needn't handle non-finite values.
Results may differ from the reference program's by a relative error of at most 0.034.
Values may be sent and summed in bfloat16 or wider, within the bound.
No kernel may reach another device: no remote copies, remote signals or barrier semaphores. Data moves between devices by JAX's collectives and lax.ppermute only.
A program may use at most 192 MiB of HBM per device.

```python
import jax
import jax.numpy as jnp
from jax import lax

HK = 16
HV = 32
DK = 128
DV = 128
SPAN = 128
LENGTH = 2048
SEQS = 8


def draw_a_log(key, part):
    key = jax.random.fold_in(key, 11)
    first = jax.random.fold_in(key, 0)
    return jax.random.uniform(first, (HV,), jnp.float32, -10.0, -3.0)


def levels(key, dims, shards, smallest, largest):
    level = 1.0
    for position, shards_of in shards:
        draws = jax.random.uniform(jax.random.fold_in(jax.random.fold_in(key, 6), position), (shards_of,), jnp.float32, smallest / len(shards), largest / len(shards))
        level = level * jnp.repeat(jnp.exp(draws), dims[position] // shards_of).reshape((-1,) + (1,) * (len(dims) - 1 - position))
    return level


def bell_draw(rng, extent, scale, most, cuts=(), kind=jnp.bfloat16):
    loudness = levels(rng, extent, cuts, -0.22, 0.18) if cuts else 1.0
    values = jax.random.normal(rng, extent, jnp.float32) * scale * loudness
    return jnp.minimum(jnp.maximum(values, -most), most).astype(kind)


def setup_inputs(seed: int = 0) -> dict:
    splits = jax.random.split(jax.random.key(seed), 11)
    query = bell_draw(splits[0], (SEQS, LENGTH, HK * DK), 1.0, 6.0, ((0, 8), (1, 16)))
    key = bell_draw(splits[1], (SEQS, LENGTH, HK * DK), 1.0, 6.0, ((0, 8), (1, 16)))
    value = bell_draw(splits[2], (SEQS, LENGTH, HV * DV), 1.0, 6.0, ((0, 8), (1, 16)))
    gate_in = bell_draw(splits[3], (SEQS, LENGTH, HV * DV), 1.0, 6.0, ((0, 8), (1, 16)))
    decay_in = bell_draw(splits[4], (SEQS, LENGTH, HV), 1.0, 6.0, ((0, 8), (1, 16)))
    beta_in = bell_draw(splits[5], (SEQS, LENGTH, HV), 1.5, 6.0, ((0, 8), (1, 16)))
    a_log = draw_a_log(jax.random.fold_in(splits[10], 71), 0)
    dt_bias = jnp.clip(jax.random.uniform(splits[7], (HV,), jnp.float32, -2.0, 1.0), -2.0, 1.0)
    norm_weight = jnp.clip(1.0 + 0.18 * jax.random.normal(splits[8], (DV,), jnp.float32), 0.1, 1.9)
    d_out = bell_draw(splits[9], (SEQS, LENGTH, HV * DV), 1.0, 6.0, ((0, 8), (1, 16)))
    return dict(query=query, key=key, value=value, gate_in=gate_in, decay_in=decay_in, beta_in=beta_in, a_log=a_log, dt_bias=dt_bias, norm_weight=norm_weight, d_out=d_out)


def delta_rule(query_h, key_h, value_h, log_decay, beta):
    length, heads, recursion_depth = query_h.shape
    width = value_h.shape[2]
    blocks = length // SPAN

    def split(array):
        return array.reshape((blocks, SPAN) + array.shape[1:])
    indices = jnp.arange(SPAN)
    below = indices[:, None] > indices[None, :]
    causal = indices[:, None] >= indices[None, :]
    identity = jnp.eye(SPAN, dtype=jnp.float32)
    highest_precision = lax.Precision.HIGHEST

    def advance(carried_state, segment_parts):
        query_rounded, key_rounded, value_block, decay_block, beta_block = segment_parts
        query_segment = query_rounded.astype(jnp.float32)
        key_segment = key_rounded.astype(jnp.float32)
        running_state = jnp.cumsum(decay_block, axis=0)
        across = running_state.T
        spread = across[:, :, None] - across[:, None, :]
        weights = jnp.where(causal, jnp.exp(jnp.where(causal, spread, 0.0)), 0.0)
        kernel = jnp.einsum('ihd,jhd->hij', key_segment, key_segment, precision=highest_precision)
        system = identity + jnp.where(below, beta_block.T[:, :, None] * kernel * weights, 0.0)
        scaled = jnp.concatenate([key_segment * (beta_block * jnp.exp(running_state))[:, :, None], value_block * beta_block[:, :, None]], axis=2)
        solved_system = jax.scipy.linalg.solve_triangular(system, jnp.transpose(scaled, (1, 0, 2)), lower=True, unit_diagonal=True)
        newest_state = solved_system[:, :, recursion_depth:] - jnp.einsum('nuy,nyl->nul', solved_system[:, :, :recursion_depth], carried_state, precision=highest_precision)
        scores = jnp.einsum('ihd,jhd->hij', query_segment, key_segment, precision=highest_precision) * weights
        output_rows = jnp.einsum('luz,uzw->luw', query_segment * jnp.exp(running_state)[:, :, None], carried_state, precision=highest_precision)
        output_rows = output_rows + jnp.einsum('hij,hjv->ihv', scores, newest_state, precision=highest_precision)
        closing_state = running_state[-1]
        carried_state = carried_state * jnp.exp(closing_state)[:, None, None] + jnp.einsum('mqp,qmb->qpb', key_segment * jnp.exp(closing_state[None, :] - running_state)[:, :, None], newest_state, precision=highest_precision)
        return (carried_state, output_rows)
    initial = jnp.zeros((heads, recursion_depth, width), jnp.float32)
    _, outputs = lax.scan(jax.checkpoint(advance), initial, (split(query_h), split(key_h), split(value_h), split(log_decay), split(beta)))
    return outputs.reshape(length, heads, width)

def mixer_core(query, key, value, decay_in, beta_in, a_log, dt_bias):
    length = query.shape[0]
    heads_key = query.shape[1] // DK
    heads_value = a_log.shape[0]
    query_h = query.reshape(length, heads_key, DK)
    key_h = key.reshape(length, heads_key, DK)
    query_h = (query_h * lax.rsqrt(lax.optimization_barrier(jnp.sum(query_h * query_h, axis=2, keepdims=True)) + 1e-06) * DK ** (-0.5)).astype(jnp.bfloat16)
    key_h = (key_h * lax.rsqrt(lax.optimization_barrier(jnp.sum(key_h * key_h, axis=2, keepdims=True)) + 1e-06)).astype(jnp.bfloat16)
    ratio = heads_value // heads_key
    query_h = jnp.repeat(query_h, ratio, axis=1)
    key_h = jnp.repeat(key_h, ratio, axis=1)
    value_h = value.reshape(length, heads_value, DV)
    log_decay = -jnp.exp(a_log) * jax.nn.softplus(decay_in + dt_bias)
    beta = jax.nn.sigmoid(beta_in)
    core = delta_rule(query_h, key_h, value_h, log_decay, beta)
    return core.reshape(length, heads_value * DV)

def gated_norm(core, gate, weight):
    shape = core.shape
    width = weight.shape[0]
    heads = core.reshape(shape[:-1] + (shape[-1] // width, width))
    gates = gate.reshape(shape[:-1] + (shape[-1] // width, width))
    scale = lax.rsqrt(lax.optimization_barrier(jnp.mean(heads * heads, axis=-1, keepdims=True)) + 1e-06)
    return (heads * scale * weight * jax.nn.silu(gates)).reshape(shape)

def reference(query, key, value, gate_in, decay_in, beta_in, a_log, dt_bias, norm_weight, d_out):

    def one_sequence(items):
        seq_query, seq_key, seq_value, seq_gate, seq_decay, seq_beta, seq_grad = items
        core, core_back = jax.vjp(mixer_core, seq_query.astype(jnp.float32), seq_key.astype(jnp.float32), seq_value.astype(jnp.float32), seq_decay.astype(jnp.float32), seq_beta.astype(jnp.float32), a_log, dt_bias)
        rounded = lax.optimization_barrier(core.astype(jnp.bfloat16))
        mixed, norm_back = jax.vjp(gated_norm, rounded.astype(jnp.float32), seq_gate.astype(jnp.float32), norm_weight)
        d_core, d_gate, d_weight = norm_back(seq_grad.astype(jnp.float32))
        d_rounded = lax.optimization_barrier(d_core.astype(jnp.bfloat16))
        grads = core_back(d_rounded.astype(jnp.float32))
        return (mixed.astype(jnp.bfloat16), grads[0].astype(jnp.bfloat16), grads[1].astype(jnp.bfloat16), grads[2].astype(jnp.bfloat16), d_gate.astype(jnp.bfloat16), grads[3].astype(jnp.bfloat16), grads[4].astype(jnp.bfloat16), grads[5], grads[6], d_weight)
    results = lax.map(one_sequence, (query, key, value, gate_in, decay_in, beta_in, d_out))
    return (results[0], results[1], results[2], results[3], results[4], results[5], results[6], lax.optimization_barrier(jnp.sum(results[7], axis=0)), lax.optimization_barrier(jnp.sum(results[8], axis=0)), lax.optimization_barrier(jnp.sum(results[9], axis=0)))
```

```python
import jax
import jax.numpy as jnp
from jax import lax
from jax.experimental import pallas as pl
from jax.experimental.pallas import tpu as pltpu
from jax.sharding import PartitionSpec as P


D = 128
HG = 4
RATIO = 2
EPS = 1e-06
F32 = jnp.float32
BF = jnp.bfloat16
HIGH = lax.Precision.HIGHEST


def nn(a, b):
    return jnp.dot(a.astype(BF), b.astype(BF), preferred_element_type=F32)


def nt(a, b):
    return lax.dot_general(
        a.astype(BF), b.astype(BF), (((1,), (1,)), ((), ())), preferred_element_type=F32
    )


def tn(a, b):
    return lax.dot_general(
        a.astype(BF), b.astype(BF), (((0,), (0,)), ((), ())), preferred_element_type=F32
    )


def fine(product, a, b):
    high_a, high_b = a.astype(BF), b.astype(BF)
    rest_a = (a - high_a.astype(F32)).astype(BF)
    rest_b = (b - high_b.astype(F32)).astype(BF)
    return product(high_a, high_b) + (product(rest_a, high_b) + product(high_a, rest_b))


def grid_index(shape, dim):
    return lax.broadcasted_iota(jnp.int32, shape, dim)


def sigmoid(x):
    return 1.0 / (1.0 + jnp.exp(-x))


def softplus(x):
    return jnp.maximum(x, 0.0) + jnp.log1p(jnp.exp(-jnp.abs(x)))


def span_weights(causal, g_col, g_row):
    return jnp.where(causal, jnp.exp(jnp.where(causal, g_col - g_row, 0.0)), 0.0)


def column(row):
    size = row.shape[1]
    here = grid_index((size, size), 0) == grid_index((size, size), 1)
    return jnp.sum(jnp.where(here, row, 0.0), axis=1, keepdims=True)


def decays(decay_ref, rate_ref, bias_ref):
    rate = -jnp.exp(column(rate_ref[...]))
    logits = decay_ref[0].astype(F32) + column(bias_ref[...])
    return rate * softplus(logits), rate * sigmoid(logits)


def first_kernel(
    q_ref, k_ref, v_ref, decay_ref, beta_ref, rate_ref, bias_ref,
    qn_ref, kn_ref, ab_ref, x_ref, wu_ref, col_ref, row_ref,
    g_all, column_all,
):
    step = pl.program_id(0)
    row, col = grid_index((D, D), 0), grid_index((D, D), 1)
    causal, below = row >= col, row > col
    diff = row ^ col
    heads = decay_ref.shape[1]
    count = HG * RATIO

    @pl.when(step == 0)
    def _():
        log_decay, _ = decays(decay_ref, rate_ref, bias_ref)
        upper = jnp.where(row <= col, 1.0, 0.0)
        g = jnp.dot(log_decay, upper, precision=HIGH, preferred_element_type=F32)
        g_all[...] = g
        beta = sigmoid(beta_ref[0].astype(F32))
        rest = jnp.zeros((D - 2 * heads, D), F32)
        column_all[...] = jnp.concatenate([g, beta, rest], axis=0).T

    cols = pltpu.roll(column_all[...], lax.rem(D - step * count, D), 1)
    rows = g_all[pl.ds(pl.multiple_of(step * count, count), count), :]
    col_ref[0] = cols
    row_ref[...] = rows
    systems, sides, ends = [], [], []
    for j in range(HG):
        part = slice(j * D, (j + 1) * D)
        q = q_ref[0, :, part].astype(F32)
        k = k_ref[0, :, part].astype(F32)
        qn = q * lax.rsqrt(jnp.sum(q * q, axis=1, keepdims=True) + EPS) * D**-0.5
        kn = (k * lax.rsqrt(jnp.sum(k * k, axis=1, keepdims=True) + EPS)).astype(BF)
        qn_ref[:, part] = qn.astype(BF)
        kn_ref[:, part] = kn
        kf = kn.astype(F32)
        gram = nt(kn, kn)
        for r in range(RATIO):
            n = j * RATIO + r
            g_col, g_row = cols[:, n : n + 1], rows[n : n + 1, :]
            beta = cols[:, heads + n : heads + n + 1]
            weights = span_weights(below, g_col, g_row)
            systems.append(beta * gram * weights)
            v = v_ref[0, :, n * D : (n + 1) * D].astype(F32)
            sides.append(jnp.concatenate([kf * (beta * jnp.exp(g_col)), v * beta], axis=1))
            last = g_row[:, D - 1 :]
            ends.append((kf * jnp.exp(last - g_col), jnp.exp(last)))
    identity = jnp.where(row == col, 1.0, 0.0)
    inverse = [identity - jnp.where(diff == 1, s, 0.0) for s in systems]
    size = 2
    while size < D:
        level = (diff >= size) & (diff < 2 * size)
        low = [x.astype(BF) for x in inverse]
        inner = [nn(jnp.where(level, systems[n], 0.0), low[n]) for n in range(count)]
        inverse = [inverse[n] - nn(low[n], inner[n]) for n in range(count)]
        size *= 2
    solved = [fine(nn, inverse[n], sides[n]) for n in range(count)]
    for n in range(count):
        x_ref[n] = inverse[n].astype(BF)
        wu_ref[n] = solved[n].astype(BF)
    closed = [fine(tn, ends[n][0], solved[n]) for n in range(count)]
    for n in range(count):
        ab_ref[n, :, :D] = (identity * ends[n][1] - closed[n][:, :D]).astype(BF)
        ab_ref[n, :, D:] = closed[n][:, D:].astype(BF)


def local_kernel(qn_ref, kn_ref, wu_ref, col_ref, row_ref, p_ref, r_ref, o_ref):
    causal = grid_index((D, D), 0) >= grid_index((D, D), 1)
    cols, rows = col_ref[0], row_ref[...]
    count = HG * RATIO
    scores = [
        nt(qn_ref[:, j * D : (j + 1) * D], kn_ref[:, j * D : (j + 1) * D]) for j in range(HG)
    ]
    for n in range(count):
        g_col, g_row = cols[:, n : n + 1], rows[n : n + 1, :]
        p_ref[n] = (scores[n // RATIO] * span_weights(causal, g_col, g_row)).astype(BF)
    both = [nn(p_ref[n], wu_ref[n]) for n in range(count)]
    for n in range(count):
        j = n // RATIO
        qn = qn_ref[:, j * D : (j + 1) * D].astype(F32)
        r_ref[n] = (qn * jnp.exp(cols[:, n : n + 1]) - both[n][:, :D]).astype(BF)
        o_ref[n] = both[n][:, D:]


def forward_scan(ab_ref, s_ref):
    chunks = ab_ref.shape[0] // RATIO
    states = [jnp.zeros((D, D), F32) for _ in range(RATIO)]
    for c in range(chunks):
        for r in range(RATIO):
            n = c * RATIO + r
            high = states[r].astype(BF)
            s_ref[n] = high
            if c == chunks - 1:
                continue
            b = ab_ref[n, :, D:].astype(F32)
            if c == 0:
                states[r] = b
                continue
            rest = (states[r] - high.astype(F32)).astype(BF)
            out = nn(ab_ref[n, :, :D], jnp.concatenate([high, rest], axis=1))
            states[r] = out[:, :D] + out[:, D:] + b


def backward_scan(ab_ref, c_ref, e_ref):
    chunks = ab_ref.shape[0] // RATIO
    states = [jnp.zeros((D, D), F32) for _ in range(RATIO)]
    for c in reversed(range(chunks)):
        for r in range(RATIO):
            n = c * RATIO + r
            high = states[r].astype(BF)
            e_ref[n] = high
            if c == 0:
                continue
            b = c_ref[n].astype(F32)
            if c == chunks - 1:
                states[r] = b
                continue
            rest = (states[r] - high.astype(F32)).astype(BF)
            out = tn(ab_ref[n, :, :D], jnp.concatenate([high, rest], axis=1))
            states[r] = out[:, :D] + out[:, D:] + b


def norm_kernel(
    r_ref, o_ref, s_ref, gate_ref, dout_ref, weight_ref,
    mixed_ref, dgate_ref, dcore_ref, c_ref, dnorm_ref,
):
    weight = weight_ref[...]

    @pl.when(pl.program_id(0) == 0)
    def _():
        dnorm_ref[...] = jnp.zeros_like(dnorm_ref)

    total = jnp.zeros((8, D), F32)
    carried = [nn(r_ref[n], s_ref[n]) for n in range(HG * RATIO)]
    for n in range(HG * RATIO):
        part = slice(n * D, (n + 1) * D)
        core = (carried[n] + o_ref[n]).astype(BF).astype(F32)
        gate = gate_ref[0, :, part].astype(F32)
        grad = dout_ref[0, :, part].astype(F32)
        scale = lax.rsqrt(jnp.mean(core * core, axis=1, keepdims=True) + EPS)
        sig = sigmoid(gate)
        silu = gate * sig
        y = core * scale
        yw = y * weight
        mixed_ref[0, :, part] = (yw * silu).astype(BF)
        dgate_ref[0, :, part] = (grad * yw * (sig * (1.0 + gate * (1.0 - sig)))).astype(BF)
        gs = grad * silu
        e = gs * weight
        ey = jnp.mean(e * y, axis=1, keepdims=True)
        dcore_ref[n] = ((e - y * ey) * scale).astype(BF)
        total = total + jnp.sum((gs * y).reshape(D // 8, 8, D), axis=0)
    dnorm_ref[...] += total
    for n in range(HG * RATIO):
        c_ref[n] = tn(r_ref[n], dcore_ref[n]).astype(BF)


def score_kernel(
    q_ref, qn_ref, kn_ref, wu_ref, p_ref, s_ref, dcore_ref, col_ref, row_ref,
    dq_ref, n_ref, dn_ref, dk_ref, drow_ref,
):
    row, col = grid_index((D, D), 0), grid_index((D, D), 1)
    causal, here = row >= col, row == col
    cols, rows = col_ref[0], row_ref[...]
    count = HG * RATIO
    taken = [nn(wu_ref[n, :, :D], s_ref[n]) for n in range(count)]
    for n in range(count):
        dn_ref[n] = tn(p_ref[n], dcore_ref[n])
        n_ref[n] = (wu_ref[n, :, D:].astype(F32) - taken[n]).astype(BF)
    both = [
        nt(dcore_ref[n], jnp.concatenate([n_ref[n], s_ref[n]], axis=0)) for n in range(count)
    ]
    dscores, dqns = [], []
    for j in range(HG):
        part = slice(j * D, (j + 1) * D)
        qf = qn_ref[:, part].astype(F32)
        dscore = jnp.zeros((D, D), F32)
        dqn = jnp.zeros((D, D), F32)
        for r in range(RATIO):
            n = j * RATIO + r
            g_col, g_row = cols[:, n : n + 1], rows[n : n + 1, :]
            dp = both[n][:, :D]
            dscore = dscore + dp * span_weights(causal, g_col, g_row)
            z = dp * p_ref[n].astype(F32)
            dqe = both[n][:, D:] * jnp.exp(g_col)
            dqn = dqn + dqe
            dg = jnp.sum(z + qf * dqe, axis=1, keepdims=True)
            drow_ref[n : n + 1, :] = jnp.sum(
                jnp.where(here, dg, 0.0) - z, axis=0, keepdims=True
            )
        dscores.append(dscore.astype(BF))
        dqns.append(dqn)
    for j in range(HG):
        part = slice(j * D, (j + 1) * D)
        dk_ref[j] = tn(dscores[j], qn_ref[:, part])
        dqn = dqns[j] + nn(dscores[j], kn_ref[:, part])
        dqn = dqn.astype(BF).astype(F32) * D**-0.5
        q = q_ref[0, :, part].astype(F32)
        inv = lax.rsqrt(jnp.sum(q * q, axis=1, keepdims=True) + EPS)
        dot = jnp.sum(q * dqn, axis=1, keepdims=True)
        dq_ref[0, :, part] = (inv * (dqn - q * (inv * inv * dot))).astype(BF)


def last_kernel(
    k_ref, v_ref, decay_ref, rate_ref, bias_ref,
    kn_ref, x_ref, wu_ref, s_ref, e_ref, n_ref, dn_ref, dk_ref, drow_ref,
    col_ref, row_ref, dnorm_ref,
    dkey_ref, dvalue_ref, ddecay_ref, dbeta_ref, sums_ref,
    dg_all, end_all, dbeta_all,
):
    step = pl.program_id(0)
    row, col = grid_index((D, D), 0), grid_index((D, D), 1)
    below, here = row > col, row == col
    heads = decay_ref.shape[1]
    count = HG * RATIO
    cols, rows = col_ref[0], row_ref[...]
    grams = [
        nt(kn_ref[:, j * D : (j + 1) * D], kn_ref[:, j * D : (j + 1) * D]) for j in range(HG)
    ]
    falls = [jnp.exp(rows[n : n + 1, D - 1 :] - cols[:, n : n + 1]) for n in range(count)]
    dns = []
    for n in range(count):
        j = n // RATIO
        kd = kn_ref[:, j * D : (j + 1) * D].astype(F32) * falls[n]
        dns.append((dn_ref[n] + nn(kd, e_ref[n])).astype(BF))
    ys = [tn(x_ref[n], dns[n]) for n in range(count)]
    boths = [
        nt(ys[n], jnp.concatenate([n_ref[n], s_ref[n]], axis=0)) for n in range(count)
    ]
    dkds = [nt(n_ref[n], e_ref[n]) for n in range(count)]
    dgrams, dkns = [], []
    for j in range(HG):
        part = slice(j * D, (j + 1) * D)
        kf = kn_ref[:, part].astype(F32)
        dgram = jnp.zeros((D, D), F32)
        dkn = dk_ref[j]
        for r in range(RATIO):
            n = j * RATIO + r
            head = step * count + n
            g_col, g_row = cols[:, n : n + 1], rows[n : n + 1, :]
            beta = cols[:, heads + n : heads + n + 1]
            weights = span_weights(below, g_col, g_row)
            rise, close = jnp.exp(g_col), jnp.exp(g_row[:, D - 1 :])
            y = ys[n]
            dlower = -boths[n][:, :D] * weights
            dside = -boths[n][:, D:] * rise
            part_beta = dlower * grams[j]
            dgram = dgram + dlower * beta
            dkd = dkds[n] * falls[n]
            kdkd = kf * dkd
            solved = jnp.sum(part_beta + kf * dside, axis=1, keepdims=True)
            sum_fall = jnp.sum(kdkd, axis=1, keepdims=True)
            dkn = dkn + dkd + dside * beta
            vpart = slice(n * D, (n + 1) * D)
            v = v_ref[0, :, vpart].astype(F32)
            dvalue_ref[0, :, vpart] = (y * beta).astype(BF)
            dbeta = solved + jnp.sum(v * y, axis=1, keepdims=True)
            dg = beta * solved - sum_fall
            dg_row = jnp.sum(jnp.where(here, dg, 0.0) - part_beta * beta, axis=0, keepdims=True)
            dg_all[pl.ds(head, 1), :] = dg_row + drow_ref[n : n + 1, :]
            product = s_ref[n].astype(F32) * e_ref[n].astype(F32) * close + kdkd
            end_all[pl.ds(head, 1), :] = jnp.sum(product, axis=0, keepdims=True)
            dbeta_all[pl.ds(head, 1), :] = jnp.sum(
                jnp.where(here, dbeta * (beta * (1.0 - beta)), 0.0), axis=0, keepdims=True
            )
        dgrams.append(dgram.astype(BF))
        dkns.append(dkn)
    for j in range(HG):
        part = slice(j * D, (j + 1) * D)
        dkn = dkns[j] + nn(dgrams[j], kn_ref[:, part]) + tn(dgrams[j], kn_ref[:, part])
        dkn = dkn.astype(BF).astype(F32)
        k = k_ref[0, :, part].astype(F32)
        inv = lax.rsqrt(jnp.sum(k * k, axis=1, keepdims=True) + EPS)
        dot = jnp.sum(k * dkn, axis=1, keepdims=True)
        dkey_ref[0, :, part] = (inv * (dkn - k * (inv * inv * dot))).astype(BF)

    @pl.when(step == pl.num_programs(0) - 1)
    def _():
        log_decay, slope = decays(decay_ref, rate_ref, bias_ref)
        lower = jnp.where(row >= col, 1.0, 0.0)
        dlog = jnp.dot(dg_all[...], lower, precision=HIGH, preferred_element_type=F32)
        dlog = dlog + jnp.sum(end_all[...], axis=1, keepdims=True)
        ddecay_ref[0] = (dlog * slope).astype(BF)
        dbeta_ref[0] = dbeta_all[...].astype(BF)
        d_rate = jnp.sum(dlog * log_decay, axis=1, keepdims=True)
        d_bias = jnp.sum(dlog * slope, axis=1, keepdims=True)
        lane = grid_index((heads, D), 1)
        own = jnp.where(lane == 0, d_rate, jnp.where(lane == 1, d_bias, 0.0))
        dnorm = jnp.sum(dnorm_ref[...], axis=0, keepdims=True)
        for j in range(heads // RATIO):
            sums_ref[j] = jnp.where(grid_index((8, D), 0) == 0, dnorm, 0.0)
            sums_ref[j, 1 : 1 + RATIO, :] = own[j * RATIO : (j + 1) * RATIO, :]


def tokens(width):
    return pl.BlockSpec((1, D, width), lambda i: (0, 0, i))


def flat(width):
    return pl.BlockSpec((D, width), lambda i: (0, i))


def lead(*shape):
    return pl.BlockSpec(shape, lambda i: (i,) + (0,) * (len(shape) - 1))


def whole(*shape):
    return pl.BlockSpec(shape, lambda i: (0,) * len(shape))


def params():
    return pltpu.CompilerParams(
        dimension_semantics=("arbitrary",), vmem_limit_bytes=60 * 1024 * 1024
    )


def cost(products, moved):
    return pl.CostEstimate(flops=products * 2 * D**3 * 8, bytes_accessed=moved, transcendentals=0)


def shards(query, key, value, gate_in, decay_in, beta_in, a_log, dt_bias, norm_weight, d_out):
    hk = query.shape[2] // D
    hv = value.shape[2] // D
    steps = hk // HG
    count = HG * RATIO
    rate, bias, weight = a_log[None], dt_bias[None], norm_weight[None]
    shape = jax.ShapeDtypeStruct
    small = whole(1, hv, D)
    decay_rows = jnp.transpose(decay_in, (0, 2, 1))
    beta_rows = jnp.transpose(beta_in, (0, 2, 1))
    columns, rows_of = lead(1, D, D), lead(count, D)
    scalars = whole(1, hv)

    qn, kn, ab, x, wu, cols, rows = pl.pallas_call(
        first_kernel,
        grid=(steps,),
        in_specs=[tokens(HG * D), tokens(HG * D), tokens(count * D), small, small, scalars, scalars],
        out_specs=[
            flat(HG * D), flat(HG * D), lead(count, D, 2 * D), lead(count, D, D),
            lead(count, D, 2 * D), columns, rows_of,
        ],
        out_shape=[
            shape((D, hk * D), BF), shape((D, hk * D), BF), shape((hv, D, 2 * D), BF),
            shape((hv, D, D), BF), shape((hv, D, 2 * D), BF), shape((steps, D, D), F32),
            shape((hv, D), F32),
        ],
        scratch_shapes=[pltpu.VMEM((hv, D), F32), pltpu.VMEM((D, D), F32)],
        compiler_params=params(),
        cost_estimate=cost(18 * hv, 8 << 20),
        name="block_solve",
    )(query, key, value, decay_rows, beta_rows, rate, bias)

    ab_owned = lax.all_to_all(ab, "seq", split_axis=0, concat_axis=0, tiled=True)

    p, r, o = pl.pallas_call(
        local_kernel,
        grid=(steps,),
        in_specs=[
            flat(HG * D), flat(HG * D), lead(count, D, 2 * D), columns, rows_of,
        ],
        out_specs=[lead(count, D, D), lead(count, D, D), lead(count, D, D)],
        out_shape=[shape((hv, D, D), BF), shape((hv, D, D), BF), shape((hv, D, D), F32)],
        compiler_params=params(),
        cost_estimate=cost(3 * hv, 8 << 20),
        name="block_scores",
    )(qn, kn, wu, cols, rows)

    s_owned = pl.pallas_call(
        forward_scan,
        out_shape=shape((hv, D, D), BF),
        compiler_params=pltpu.CompilerParams(vmem_limit_bytes=60 * 1024 * 1024),
        cost_estimate=cost(2 * hv, 3 << 20),
        name="state_scan",
    )(ab_owned)
    s = lax.all_to_all(s_owned, "seq", split_axis=0, concat_axis=0, tiled=True)

    mixed, d_gate, d_core, c, d_norm = pl.pallas_call(
        norm_kernel,
        grid=(steps,),
        in_specs=[
            lead(count, D, D), lead(count, D, D), lead(count, D, D), tokens(count * D),
            tokens(count * D), whole(1, D),
        ],
        out_specs=[
            tokens(count * D), tokens(count * D), lead(count, D, D), lead(count, D, D), whole(8, D),
        ],
        out_shape=[
            shape((1, D, hv * D), BF), shape((1, D, hv * D), BF), shape((hv, D, D), BF),
            shape((hv, D, D), BF), shape((8, D), F32),
        ],
        compiler_params=params(),
        cost_estimate=cost(2 * hv, 10 << 20),
        name="gated_norm",
    )(r, o, s, gate_in, d_out, weight)

    c_owned = lax.all_to_all(c, "seq", split_axis=0, concat_axis=0, tiled=True)

    d_query, newest, dn, dk, drow = pl.pallas_call(
        score_kernel,
        grid=(steps,),
        in_specs=[
            tokens(HG * D), flat(HG * D), flat(HG * D), lead(count, D, 2 * D), lead(count, D, D),
            lead(count, D, D), lead(count, D, D), columns, rows_of,
        ],
        out_specs=[
            tokens(HG * D), lead(count, D, D), lead(count, D, D), lead(HG, D, D), rows_of,
        ],
        out_shape=[
            shape((1, D, hk * D), BF), shape((hv, D, D), BF), shape((hv, D, D), F32),
            shape((hk, D, D), F32), shape((hv, D), F32),
        ],
        compiler_params=params(),
        cost_estimate=cost(6 * hv, 12 << 20),
        name="score_grads",
    )(query, qn, kn, wu, p, s, d_core, cols, rows)

    e_owned = pl.pallas_call(
        backward_scan,
        out_shape=shape((hv, D, D), BF),
        compiler_params=pltpu.CompilerParams(vmem_limit_bytes=60 * 1024 * 1024),
        cost_estimate=cost(2 * hv, 4 << 20),
        name="state_grad_scan",
    )(ab_owned, c_owned)
    e = lax.all_to_all(e_owned, "seq", split_axis=0, concat_axis=0, tiled=True)

    d_key, d_value, d_decay, d_beta, sums = pl.pallas_call(
        last_kernel,
        grid=(steps,),
        in_specs=[
            tokens(HG * D), tokens(count * D), small, scalars, scalars,
            flat(HG * D), lead(count, D, D), lead(count, D, 2 * D), lead(count, D, D),
            lead(count, D, D), lead(count, D, D), lead(count, D, D), lead(HG, D, D),
            rows_of, columns, rows_of, whole(8, D),
        ],
        out_specs=[tokens(HG * D), tokens(count * D), small, small, whole(hk, 8, D)],
        out_shape=[
            shape((1, D, hk * D), BF), shape((1, D, hv * D), BF), shape((1, hv, D), BF),
            shape((1, hv, D), BF), shape((hk, 8, D), F32),
        ],
        scratch_shapes=[pltpu.VMEM((hv, D), F32)] * 3,
        compiler_params=params(),
        cost_estimate=cost(8 * hv, 14 << 20),
        name="solve_grads",
    )(
        key, value, decay_rows, rate, bias, kn, x, wu, s, e, newest, dn, dk, drow, cols, rows,
        d_norm,
    )

    sums = lax.all_to_all(sums, "seq", split_axis=0, concat_axis=0, tiled=True)
    sums = jnp.sum(sums, axis=0)
    size = lax.axis_size("dp")
    hop = 1
    while hop < size:
        sums = sums + lax.ppermute(sums, "dp", [(i, i ^ hop) for i in range(size)])
        hop *= 2
    return (
        mixed, d_query, d_key, d_value, d_gate,
        jnp.transpose(d_decay, (0, 2, 1)), jnp.transpose(d_beta, (0, 2, 1)),
        sums[1 : 1 + RATIO, 0], sums[1 : 1 + RATIO, 1], sums[0],
    )


def solution(mesh):
    row = P("dp", "seq", None)
    return jax.shard_map(
        shards,
        mesh=mesh,
        in_specs=(row, row, row, row, row, row, P(), P(), P(), row),
        out_specs=(row, row, row, row, row, row, row, P("seq"), P("seq"), P()),
        check_vma=False,
    )
```

```python
import jax
import jax.numpy as jnp
from jax import lax
from jax.experimental import pallas as pl
from jax.experimental.pallas import tpu as pltpu
from jax.sharding import PartitionSpec as P


D = 128
HG = 4
RATIO = 2
EPS = 1e-06
F32 = jnp.float32
BF = jnp.bfloat16
HIGH = lax.Precision.HIGHEST


def nn(a, b):
    return jnp.dot(a.astype(BF), b.astype(BF), preferred_element_type=F32)


def nt(a, b):
    return lax.dot_general(
        a.astype(BF), b.astype(BF), (((1,), (1,)), ((), ())), preferred_element_type=F32
    )


def tn(a, b):
    return lax.dot_general(
        a.astype(BF), b.astype(BF), (((0,), (0,)), ((), ())), preferred_element_type=F32
    )


def parts(a):
    high = a.astype(BF)
    return high, (a - high.astype(F32)).astype(BF)


def fine_tn(a, b):
    high_a, rest_a = parts(a)
    high_b, rest_b = parts(b)
    both = tn(jnp.concatenate([high_a, rest_a], axis=0), jnp.concatenate([high_b, high_b], axis=0))
    return both + tn(high_a, rest_b)


def grid_index(shape, dim):
    return lax.broadcasted_iota(jnp.int32, shape, dim)


def sigmoid(x):
    return 1.0 / (1.0 + jnp.exp(-x))


def softplus(x):
    return jnp.maximum(x, 0.0) + jnp.log1p(jnp.exp(-jnp.abs(x)))


def span_weights(causal, g_col, g_row):
    return jnp.where(causal, jnp.exp(jnp.where(causal, g_col - g_row, 0.0)), 0.0)


def column(row):
    size = row.shape[1]
    here = grid_index((size, size), 0) == grid_index((size, size), 1)
    return jnp.sum(jnp.where(here, row, 0.0), axis=1, keepdims=True)


def decays(decay_ref, rate_ref, bias_ref):
    rate = -jnp.exp(column(rate_ref[...]))
    logits = decay_ref[0].astype(F32) + column(bias_ref[...])
    return rate * softplus(logits), rate * sigmoid(logits)


def natural(step, core_ref, half):
    late = step >= half
    core = core_ref[0]
    return jnp.where(late, core, 1 - core) * half + jnp.where(late, step - half, step)


def store_half(early, send_ref, keep_ref, values):
    @pl.when(early)
    def _():
        for n, value in enumerate(values):
            send_ref[n] = value

    @pl.when(jnp.logical_not(early))
    def _():
        for n, value in enumerate(values):
            keep_ref[n] = value


def first_kernel(
    core_ref, k_ref, v_ref, decay_ref, beta_ref, rate_ref, bias_ref,
    kn_ref, send_ref, keep_ref, x_ref, wu_ref, col_ref, row_ref,
    g_all, column_all,
):
    step = pl.program_id(0)
    row, col = grid_index((D, D), 0), grid_index((D, D), 1)
    causal, below = row >= col, row > col
    diff = row ^ col
    heads = decay_ref.shape[1]
    count = HG * RATIO

    @pl.when(step == 0)
    def _():
        log_decay, _ = decays(decay_ref, rate_ref, bias_ref)
        upper = jnp.where(row <= col, 1.0, 0.0)
        g = jnp.dot(log_decay, upper, precision=HIGH, preferred_element_type=F32)
        g_all[...] = g
        beta = sigmoid(beta_ref[0].astype(F32))
        rest = jnp.zeros((D - 2 * heads, D), F32)
        column_all[...] = jnp.concatenate([g, beta, rest], axis=0).T

    half = pl.num_programs(0) // 2
    start = natural(step, core_ref, half) * count
    cols = pltpu.roll(column_all[...], lax.rem(D - start, D), 1)
    rows = g_all[pl.ds(pl.multiple_of(start, count), count), :]
    col_ref[0] = cols
    row_ref[...] = rows
    systems, sides, ends = [], [], []
    for j in range(HG):
        part = slice(j * D, (j + 1) * D)
        k = k_ref[0, :, part].astype(F32)
        kn = (k * lax.rsqrt(jnp.sum(k * k, axis=1, keepdims=True) + EPS)).astype(BF)
        kn_ref[:, part] = kn
        kf = kn.astype(F32)
        gram = nt(kn, kn)
        for r in range(RATIO):
            n = j * RATIO + r
            g_col, g_row = cols[:, n : n + 1], rows[n : n + 1, :]
            beta = cols[:, heads + n : heads + n + 1]
            weights = span_weights(below, g_col, g_row)
            systems.append(beta * gram * weights)
            v = v_ref[0, :, n * D : (n + 1) * D].astype(F32)
            sides.append(jnp.concatenate([kf * (beta * jnp.exp(g_col)), v * beta], axis=1))
            last = g_row[:, D - 1 :]
            ends.append((kf * jnp.exp(last - g_col), jnp.exp(last)))
    identity = jnp.where(row == col, 1.0, 0.0)
    inverse = [identity - jnp.where(diff == 1, s, 0.0) for s in systems]
    size = 2
    while size < D:
        level = (diff >= size) & (diff < 2 * size)
        low = [x.astype(BF) for x in inverse]
        inner = [nn(jnp.where(level, systems[n], 0.0), low[n]) for n in range(count)]
        inverse = [inverse[n] - nn(low[n], inner[n]) for n in range(count)]
        size *= 2
    solved = [nn(inverse[n], sides[n]) for n in range(count)]
    for n in range(count):
        x_ref[n] = inverse[n].astype(BF)
        wu_ref[n] = solved[n].astype(BF)
    closed = [fine_tn(ends[n][0], solved[n]) for n in range(count)]
    maps = [
        jnp.concatenate(
            [(identity * ends[n][1] - closed[n][:, :D]).astype(BF), closed[n][:, D:].astype(BF)], axis=1
        )
        for n in range(count)
    ]
    store_half(step < half, send_ref, keep_ref, maps)


def local_kernel(
    core_ref, q_ref, kn_ref, wu_ref, col_ref, row_ref, qn_ref, p_ref, r_ref, o_ref, mark_ref
):
    mark_ref[...] = jnp.zeros_like(mark_ref)
    causal = grid_index((D, D), 0) >= grid_index((D, D), 1)
    cols, rows = col_ref[0], row_ref[...]
    count = HG * RATIO
    for j in range(HG):
        part = slice(j * D, (j + 1) * D)
        q = q_ref[0, :, part].astype(F32)
        qn = q * lax.rsqrt(jnp.sum(q * q, axis=1, keepdims=True) + EPS) * D**-0.5
        qn_ref[:, part] = qn.astype(BF)
    scores = [
        nt(qn_ref[:, j * D : (j + 1) * D], kn_ref[:, j * D : (j + 1) * D]) for j in range(HG)
    ]
    for n in range(count):
        g_col, g_row = cols[:, n : n + 1], rows[n : n + 1, :]
        p_ref[n] = (scores[n // RATIO] * span_weights(causal, g_col, g_row)).astype(BF)
    both = [nn(p_ref[n], wu_ref[n]) for n in range(count)]
    for n in range(count):
        j = n // RATIO
        qn = qn_ref[:, j * D : (j + 1) * D].astype(F32)
        r_ref[n] = (qn * jnp.exp(cols[:, n : n + 1]) - both[n][:, :D]).astype(BF)
        o_ref[n] = both[n][:, D:]


def merge_maps(core_ref, keep_ref, got_ref, out_ref):
    first = core_ref[0] == 0
    for n in range(out_ref.shape[0]):
        keep, got = keep_ref[n].astype(F32), got_ref[n].astype(F32)
        before, after = jnp.where(first, keep, got), jnp.where(first, got, keep)
        out = nn(after[:, :D], before)
        out_ref[n, :, :D] = out[:, :D].astype(BF)
        out_ref[n, :, D:] = (out[:, D:] + after[:, D:]).astype(BF)


def place_states(core_ref, keep_ref, got_ref, start_ref, own_ref, send_ref):
    first = core_ref[0] == 0
    for n in range(start_ref.shape[0]):
        before = jnp.where(first, keep_ref[n].astype(F32), got_ref[n].astype(F32))
        start = start_ref[n].astype(F32)
        later = nn(before[:, :D], start) + before[:, D:]
        own_ref[n] = jnp.where(first, start, later).astype(BF)
        send_ref[n] = jnp.where(first, later, start).astype(BF)


def merge_sources(core_ref, keep_ref, got_ref, keep_c_ref, got_c_ref, out_ref):
    first = core_ref[0] == 0
    for n in range(out_ref.shape[0]):
        before = jnp.where(first, keep_ref[n].astype(F32), got_ref[n].astype(F32))
        keep, got = keep_c_ref[n].astype(F32), got_c_ref[n].astype(F32)
        early, late = jnp.where(first, keep, got), jnp.where(first, got, keep)
        out_ref[n] = (early + tn(before[:, :D], late)).astype(BF)


def place_grads(
    core_ref, keep_ref, got_ref, keep_c_ref, got_c_ref, end_ref, own_ref, send_ref
):
    first = core_ref[0] == 0
    for n in range(end_ref.shape[0]):
        after = jnp.where(first, got_ref[n].astype(F32), keep_ref[n].astype(F32))
        late = jnp.where(first, got_c_ref[n].astype(F32), keep_c_ref[n].astype(F32))
        end = end_ref[n].astype(F32)
        middle = late + tn(after[:, :D], end)
        own_ref[n] = jnp.where(first, middle, end).astype(BF)
        send_ref[n] = jnp.where(first, end, middle).astype(BF)


def forward_scan(ab_ref, _, s_ref):
    chunks = ab_ref.shape[0] // RATIO
    states = [jnp.zeros((D, D), F32) for _ in range(RATIO)]
    for c in range(chunks):
        for r in range(RATIO):
            n = c * RATIO + r
            high = states[r].astype(BF)
            s_ref[n] = high
            if c == chunks - 1:
                continue
            b = ab_ref[n, :, D:].astype(F32)
            if c == 0:
                states[r] = b
                continue
            rest = (states[r] - high.astype(F32)).astype(BF)
            out = nn(ab_ref[n, :, :D], jnp.concatenate([high, rest], axis=1))
            states[r] = out[:, :D] + out[:, D:] + b


def backward_scan(ab_ref, c_ref, _, e_ref):
    chunks = ab_ref.shape[0] // RATIO
    states = [jnp.zeros((D, D), F32) for _ in range(RATIO)]
    for c in reversed(range(chunks)):
        for r in range(RATIO):
            n = c * RATIO + r
            high = states[r].astype(BF)
            e_ref[n] = high
            if c == 0:
                continue
            b = c_ref[n].astype(F32)
            if c == chunks - 1:
                states[r] = b
                continue
            rest = (states[r] - high.astype(F32)).astype(BF)
            out = tn(ab_ref[n, :, :D], jnp.concatenate([high, rest], axis=1))
            states[r] = out[:, :D] + out[:, D:] + b


def norm_kernel(
    core_ref, r_ref, o_ref, got_ref, own_ref, gate_ref, dout_ref, weight_ref,
    mixed_ref, dgate_ref, dcore_ref, s_ref, send_ref, keep_ref, dnorm_ref,
):
    weight = weight_ref[...]
    early = pl.program_id(0) < pl.num_programs(0) // 2

    @pl.when(early)
    def _():
        s_ref[...] = got_ref[...]

    @pl.when(jnp.logical_not(early))
    def _():
        s_ref[...] = own_ref[...]

    @pl.when(pl.program_id(0) == 0)
    def _():
        dnorm_ref[...] = jnp.zeros_like(dnorm_ref)

    total = jnp.zeros((8, D), F32)
    carried = [nn(r_ref[n], s_ref[n]) for n in range(HG * RATIO)]
    for n in range(HG * RATIO):
        part = slice(n * D, (n + 1) * D)
        core = (carried[n] + o_ref[n]).astype(BF).astype(F32)
        gate = gate_ref[0, :, part].astype(F32)
        grad = dout_ref[0, :, part].astype(F32)
        scale = lax.rsqrt(jnp.mean(core * core, axis=1, keepdims=True) + EPS)
        sig = sigmoid(gate)
        silu = gate * sig
        y = core * scale
        yw = y * weight
        mixed_ref[0, :, part] = (yw * silu).astype(BF)
        dgate_ref[0, :, part] = (grad * yw * (sig * (1.0 + gate * (1.0 - sig)))).astype(BF)
        gs = grad * silu
        e = gs * weight
        ey = jnp.mean(e * y, axis=1, keepdims=True)
        dcore_ref[n] = ((e - y * ey) * scale).astype(BF)
        total = total + jnp.sum((gs * y).reshape(D // 8, 8, D), axis=0)
    dnorm_ref[...] += total
    sources = [tn(r_ref[n], dcore_ref[n]).astype(BF) for n in range(HG * RATIO)]
    store_half(early, send_ref, keep_ref, sources)


def score_kernel(
    core_ref, q_ref, qn_ref, kn_ref, wu_ref, x_ref, p_ref, s_ref, dcore_ref, col_ref, row_ref,
    dq_ref, n_ref, y_ref, xk_ref, gram_ref, dk_ref, drow_ref,
):
    row, col = grid_index((D, D), 0), grid_index((D, D), 1)
    causal, here = row >= col, row == col
    cols, rows = col_ref[0], row_ref[...]
    count = HG * RATIO
    taken = [nn(wu_ref[n, :, :D], s_ref[n]) for n in range(count)]
    for n in range(count):
        n_ref[n] = (wu_ref[n, :, D:].astype(F32) - taken[n]).astype(BF)
    both = [
        nt(dcore_ref[n], jnp.concatenate([n_ref[n], s_ref[n]], axis=0)) for n in range(count)
    ]
    dns = [tn(p_ref[n], dcore_ref[n]).astype(BF) for n in range(count)]
    for n in range(count):
        part = slice(n // RATIO * D, (n // RATIO + 1) * D)
        fall = jnp.exp(rows[n : n + 1, D - 1 :] - cols[:, n : n + 1])
        kd = (kn_ref[:, part].astype(F32) * fall).astype(BF)
        out = tn(x_ref[n], jnp.concatenate([dns[n], kd], axis=1))
        y_ref[n] = out[:, :D]
        xk_ref[n] = out[:, D:].astype(BF)
    for j in range(HG):
        part = slice(j * D, (j + 1) * D)
        gram_ref[j] = nt(kn_ref[:, part], kn_ref[:, part])
    dscores, dqns = [], []
    for j in range(HG):
        part = slice(j * D, (j + 1) * D)
        qf = qn_ref[:, part].astype(F32)
        dscore = jnp.zeros((D, D), F32)
        dqn = jnp.zeros((D, D), F32)
        for r in range(RATIO):
            n = j * RATIO + r
            g_col, g_row = cols[:, n : n + 1], rows[n : n + 1, :]
            dp = both[n][:, :D]
            dscore = dscore + dp * span_weights(causal, g_col, g_row)
            z = dp * p_ref[n].astype(F32)
            dqe = both[n][:, D:] * jnp.exp(g_col)
            dqn = dqn + dqe
            dg = jnp.sum(z + qf * dqe, axis=1, keepdims=True)
            drow_ref[n : n + 1, :] = jnp.sum(
                jnp.where(here, dg, 0.0) - z, axis=0, keepdims=True
            )
        dscores.append(dscore.astype(BF))
        dqns.append(dqn)
    for j in range(HG):
        part = slice(j * D, (j + 1) * D)
        dk_ref[j] = tn(dscores[j], qn_ref[:, part])
        dqn = dqns[j] + nn(dscores[j], kn_ref[:, part])
        dqn = dqn.astype(BF).astype(F32) * D**-0.5
        q = q_ref[0, :, part].astype(F32)
        inv = lax.rsqrt(jnp.sum(q * q, axis=1, keepdims=True) + EPS)
        dot = jnp.sum(q * dqn, axis=1, keepdims=True)
        dq_ref[0, :, part] = (inv * (dqn - q * (inv * inv * dot))).astype(BF)


def last_kernel(
    core_ref, k_ref, v_ref, decay_ref, rate_ref, bias_ref,
    kn_ref, s_ref, got_ref, own_ref, n_ref, y_ref, xk_ref, gram_ref, dk_ref, drow_ref,
    col_ref, row_ref, dnorm_ref,
    dkey_ref, dvalue_ref, ddecay_ref, dbeta_ref, sums_ref,
    dg_all, end_all, dbeta_all, e_ref,
):
    step = pl.program_id(0)
    row, col = grid_index((D, D), 0), grid_index((D, D), 1)
    below, here = row > col, row == col
    heads = decay_ref.shape[1]
    count = HG * RATIO
    cols, rows = col_ref[0], row_ref[...]
    half = pl.num_programs(0) // 2
    start = natural(step, core_ref, half) * count

    @pl.when(step < half)
    def _():
        e_ref[...] = got_ref[...]

    @pl.when(step >= half)
    def _():
        e_ref[...] = own_ref[...]

    falls = [jnp.exp(rows[n : n + 1, D - 1 :] - cols[:, n : n + 1]) for n in range(count)]
    ys = [y_ref[n] + nn(xk_ref[n], e_ref[n]) for n in range(count)]
    boths = [
        nt(ys[n], jnp.concatenate([n_ref[n], s_ref[n]], axis=0)) for n in range(count)
    ]
    dkds = [nt(n_ref[n], e_ref[n]) for n in range(count)]
    dgrams, dkns = [], []
    for j in range(HG):
        part = slice(j * D, (j + 1) * D)
        kf = kn_ref[:, part].astype(F32)
        dgram = jnp.zeros((D, D), F32)
        dkn = dk_ref[j]
        for r in range(RATIO):
            n = j * RATIO + r
            head = start + n
            g_col, g_row = cols[:, n : n + 1], rows[n : n + 1, :]
            beta = cols[:, heads + n : heads + n + 1]
            weights = span_weights(below, g_col, g_row)
            rise, close = jnp.exp(g_col), jnp.exp(g_row[:, D - 1 :])
            y = ys[n]
            dlower = -boths[n][:, :D] * weights
            dside = -boths[n][:, D:] * rise
            part_beta = dlower * gram_ref[j]
            dgram = dgram + dlower * beta
            dkd = dkds[n] * falls[n]
            kdkd = kf * dkd
            solved = jnp.sum(part_beta + kf * dside, axis=1, keepdims=True)
            sum_fall = jnp.sum(kdkd, axis=1, keepdims=True)
            dkn = dkn + dkd + dside * beta
            vpart = slice(n * D, (n + 1) * D)
            v = v_ref[0, :, vpart].astype(F32)
            dvalue_ref[0, :, vpart] = (y * beta).astype(BF)
            dbeta = solved + jnp.sum(v * y, axis=1, keepdims=True)
            dg = beta * solved - sum_fall
            dg_row = jnp.sum(jnp.where(here, dg, 0.0) - part_beta * beta, axis=0, keepdims=True)
            dg_all[pl.ds(head, 1), :] = dg_row + drow_ref[n : n + 1, :]
            product = s_ref[n].astype(F32) * e_ref[n].astype(F32) * close + kdkd
            end_all[pl.ds(head, 1), :] = jnp.sum(product, axis=0, keepdims=True)
            dbeta_all[pl.ds(head, 1), :] = jnp.sum(
                jnp.where(here, dbeta * (beta * (1.0 - beta)), 0.0), axis=0, keepdims=True
            )
        dgrams.append(dgram.astype(BF))
        dkns.append(dkn)
    for j in range(HG):
        part = slice(j * D, (j + 1) * D)
        dkn = dkns[j] + nn(dgrams[j], kn_ref[:, part]) + tn(dgrams[j], kn_ref[:, part])
        dkn = dkn.astype(BF).astype(F32)
        k = k_ref[0, :, part].astype(F32)
        inv = lax.rsqrt(jnp.sum(k * k, axis=1, keepdims=True) + EPS)
        dot = jnp.sum(k * dkn, axis=1, keepdims=True)
        dkey_ref[0, :, part] = (inv * (dkn - k * (inv * inv * dot))).astype(BF)

    @pl.when(step == pl.num_programs(0) - 1)
    def _():
        log_decay, slope = decays(decay_ref, rate_ref, bias_ref)
        lower = jnp.where(row >= col, 1.0, 0.0)
        dlog = jnp.dot(dg_all[...], lower, precision=HIGH, preferred_element_type=F32)
        dlog = dlog + jnp.sum(end_all[...], axis=1, keepdims=True)
        ddecay_ref[0] = (dlog * slope).astype(BF)
        dbeta_ref[0] = dbeta_all[...].astype(BF)
        d_rate = jnp.sum(dlog * log_decay, axis=1, keepdims=True)
        d_bias = jnp.sum(dlog * slope, axis=1, keepdims=True)
        lane = grid_index((heads, D), 1)
        which = lax.rem(grid_index((heads, D), 0), RATIO)
        own = jnp.where(lane == which, d_rate, jnp.where(lane == RATIO + which, d_bias, 0.0))
        dnorm = jnp.sum(dnorm_ref[...], axis=0, keepdims=True)
        groups = heads // RATIO
        copies = sums_ref.shape[0] // groups
        for j in range(groups):
            both = jnp.sum(own[j * RATIO : (j + 1) * RATIO, :], axis=0, keepdims=True)
            both = jnp.where(grid_index((2, D), 0) == 0, dnorm, both)
            sums_ref[pl.ds(j * copies, copies)] = jnp.broadcast_to(both[None], (copies, 2, D))


def params(room):
    return pltpu.CompilerParams(
        dimension_semantics=("arbitrary",), vmem_limit_bytes=room * 1024 * 1024
    )


def cost(products, moved):
    return pl.CostEstimate(flops=products * 2 * D**3 * 8, bytes_accessed=moved, transcendentals=0)


def shards(query, key, value, gate_in, decay_in, beta_in, a_log, dt_bias, norm_weight, d_out):
    hk = query.shape[2] // D
    hv = value.shape[2] // D
    steps = hk // HG
    half = steps // 2
    count = HG * RATIO
    owned = hv // 2
    rate, bias, weight = a_log[None], dt_bias[None], norm_weight[None]
    decay_rows = jnp.transpose(decay_in, (0, 2, 1))
    beta_rows = jnp.transpose(beta_in, (0, 2, 1))
    ranks = lax.axis_size("seq")
    copies = lax.axis_size("dp")
    core = lax.rem(lax.axis_index("seq"), 2).astype(jnp.int32)[None]
    shape = jax.ShapeDtypeStruct

    def tokens(width):
        return pl.BlockSpec((1, D, width), lambda i, c: (0, 0, natural(i, c, half)))

    def flat(width):
        return pl.BlockSpec((D, width), lambda i, c: (0, i))

    def lead(*dims):
        return pl.BlockSpec(dims, lambda i, c: (i,) + (0,) * (len(dims) - 1))

    def sent(*dims):
        return pl.BlockSpec(dims, lambda i, c: (jnp.minimum(i, half - 1),) + (0,) * (len(dims) - 1))

    def kept(*dims):
        return pl.BlockSpec(dims, lambda i, c: (jnp.maximum(i - half, 0),) + (0,) * (len(dims) - 1))

    def whole(*dims):
        return pl.BlockSpec(dims, lambda i, c: (0,) * len(dims))

    def call(kernel, grid, ins, outs, out_shape, spent, name, scratch=(), room=56):
        return pl.pallas_call(
            kernel,
            grid_spec=pltpu.PrefetchScalarGridSpec(
                num_scalar_prefetch=1, grid=(grid,), in_specs=ins, out_specs=outs,
                scratch_shapes=list(scratch),
            ),
            out_shape=out_shape,
            compiler_params=params(room),
            cost_estimate=spent,
            name=name,
        )

    def to_owners(array):
        groups = [list(range(c, ranks, 2)) for c in range(2)]
        return lax.all_to_all(
            array, "seq", split_axis=0, concat_axis=0, axis_index_groups=groups, tiled=True
        )

    def to_sibling(array):
        return lax.ppermute(array, "seq", [(i, i ^ 1) for i in range(ranks)])

    small, scalars = whole(1, hv, D), whole(1, hv)
    columns, rows_of = lead(1, D, D), lead(count, D)
    square, wide = lead(count, D, D), lead(count, D, 2 * D)
    half_square, half_wide = shape((owned, D, D), BF), shape((owned, D, 2 * D), BF)
    merges = owned // count
    vmem, anywhere = pl.BlockSpec(memory_space=pltpu.VMEM), pl.BlockSpec(memory_space=pl.ANY)

    kn, ab_send, ab, x, wu, cols, rows = call(
        first_kernel,
        steps,
        [tokens(HG * D), tokens(count * D), small, small, scalars, scalars],
        [
            flat(HG * D), sent(count, D, 2 * D), kept(count, D, 2 * D), square, wide,
            columns, rows_of,
        ],
        [
            shape((D, hk * D), BF), half_wide, half_wide,
            shape((hv, D, D), BF), shape((hv, D, 2 * D), BF), shape((steps, D, D), F32),
            shape((hv, D), F32),
        ],
        cost(18 * hv, 8 << 20),
        "block_solve",
        [pltpu.VMEM((hv, D), F32), pltpu.VMEM((D, D), F32)],
    )(core, key, value, decay_rows, beta_rows, rate, bias)

    ab_got = to_sibling(ab_send)
    merged = call(
        merge_maps, merges, [wide, wide], wide, half_wide, cost(owned, 3 << 20), "merge_maps", room=24
    )(core, ab, ab_got)
    ab_owned = to_owners(merged)

    qn, p, r, o, mark = call(
        local_kernel,
        steps,
        [tokens(HG * D), flat(HG * D), wide, columns, rows_of],
        [flat(HG * D), square, square, square, whole(8, D)],
        [
            shape((D, hk * D), BF), shape((hv, D, D), BF), shape((hv, D, D), BF),
            shape((hv, D, D), F32), shape((8, D), F32),
        ],
        cost(3 * hv, 8 << 20),
        "block_scores",
    )(core, query, kn, wu, cols, rows)

    s_owned = pl.pallas_call(
        forward_scan,
        in_specs=[vmem, anywhere],
        out_shape=half_square,
        compiler_params=pltpu.CompilerParams(vmem_limit_bytes=16 * 1024 * 1024),
        cost_estimate=cost(hv, 2 << 20),
        name="state_scan",
    )(ab_owned, mark)
    s_start = to_owners(s_owned)
    s_own, s_send = call(
        place_states, merges, [wide, wide, square], [square, square], [half_square, half_square],
        cost(owned, 3 << 20), "place_states", room=24,
    )(core, ab, ab_got, s_start)
    s_got = to_sibling(s_send)

    mixed, d_gate, d_core, s, c_send, c, d_norm = call(
        norm_kernel,
        steps,
        [
            square, square, sent(count, D, D), kept(count, D, D), tokens(count * D),
            tokens(count * D), whole(1, D),
        ],
        [
            tokens(count * D), tokens(count * D), square, square, sent(count, D, D),
            kept(count, D, D), whole(8, D),
        ],
        [
            shape((1, D, hv * D), BF), shape((1, D, hv * D), BF), shape((hv, D, D), BF),
            shape((hv, D, D), BF), half_square, half_square, shape((8, D), F32),
        ],
        cost(2 * hv, 10 << 20),
        "gated_norm", room=48,
    )(core, r, o, s_got, s_own, gate_in, d_out, weight)

    c_got = to_sibling(c_send)
    c_merged = call(
        merge_sources, merges, [wide, wide, square, square], square, half_square,
        cost(owned, 3 << 20), "merge_sources", room=24,
    )(core, ab, ab_got, c, c_got)
    c_owned = to_owners(c_merged)

    d_query, newest, y, xk, gram, dk, drow = call(
        score_kernel,
        steps,
        [
            tokens(HG * D), flat(HG * D), flat(HG * D), wide, square, square, square, square,
            columns, rows_of,
        ],
        [
            tokens(HG * D), square, square, square, lead(HG, D, D), lead(HG, D, D), rows_of,
        ],
        [
            shape((1, D, hk * D), BF), shape((hv, D, D), BF), shape((hv, D, D), F32),
            shape((hv, D, D), BF), shape((hk, D, D), F32), shape((hk, D, D), F32),
            shape((hv, D), F32),
        ],
        cost(6 * hv, 12 << 20),
        "score_grads",
    )(core, query, qn, kn, wu, x, p, s, d_core, cols, rows)

    e_owned = pl.pallas_call(
        backward_scan,
        in_specs=[vmem, vmem, anywhere],
        out_shape=half_square,
        compiler_params=pltpu.CompilerParams(vmem_limit_bytes=16 * 1024 * 1024),
        cost_estimate=cost(hv, 2 << 20),
        name="state_grad_scan",
    )(ab_owned, c_owned, drow)
    e_end = to_owners(e_owned)
    e_own, e_send = call(
        place_grads, merges, [wide, wide, square, square, square], [square, square],
        [half_square, half_square], cost(owned, 4 << 20), "place_grads", room=24,
    )(core, ab, ab_got, c, c_got, e_end)
    e_got = to_sibling(e_send)

    d_key, d_value, d_decay, d_beta, sums = call(
        last_kernel,
        steps,
        [
            tokens(HG * D), tokens(count * D), small, scalars, scalars, flat(HG * D), square,
            sent(count, D, D), kept(count, D, D), square, square, square, lead(HG, D, D),
            lead(HG, D, D), rows_of, columns, rows_of, whole(8, D),
        ],
        [tokens(HG * D), tokens(count * D), small, small, whole(ranks * copies, 2, D)],
        [
            shape((1, D, hk * D), BF), shape((1, D, hv * D), BF), shape((1, hv, D), BF),
            shape((1, hv, D), BF), shape((ranks * copies, 2, D), F32),
        ],
        cost(8 * hv, 14 << 20),
        "solve_grads", room=48,
        scratch=[pltpu.VMEM((hv, D), F32)] * 3 + [pltpu.VMEM((count, D, D), BF)],
    )(
        core, key, value, decay_rows, rate, bias, kn, s, e_got, e_own, newest, y, xk, gram, dk, drow,
        cols, rows, d_norm,
    )

    sums = lax.all_to_all(sums, ("seq", "dp"), split_axis=0, concat_axis=0, tiled=True)
    sums = jnp.sum(sums, axis=0)
    return (
        mixed, d_query, d_key, d_value, d_gate,
        jnp.transpose(d_decay, (0, 2, 1)), jnp.transpose(d_beta, (0, 2, 1)),
        sums[1, :RATIO], sums[1, RATIO : 2 * RATIO], sums[0],
    )


def solution(mesh):
    row = P("dp", "seq", None)
    return jax.shard_map(
        shards,
        mesh=mesh,
        in_specs=(row, row, row, row, row, row, P(), P(), P(), row),
        out_specs=(row, row, row, row, row, row, row, P("seq"), P("seq"), P()),
        check_vma=False,
    )
```

```python
import jax
import jax.numpy as jnp
from jax import lax
from jax.experimental import pallas as pl
from jax.experimental.pallas import tpu as pltpu
from jax.sharding import PartitionSpec as P


D = 128
HG = 4
RATIO = 2
EPS = 1e-06
F32 = jnp.float32
BF = jnp.bfloat16
HIGH = lax.Precision.HIGHEST


def nn(a, b):
    return jnp.dot(a.astype(BF), b.astype(BF), preferred_element_type=F32)


def nt(a, b):
    return lax.dot_general(
        a.astype(BF), b.astype(BF), (((1,), (1,)), ((), ())), preferred_element_type=F32
    )


def tn(a, b):
    return lax.dot_general(
        a.astype(BF), b.astype(BF), (((0,), (0,)), ((), ())), preferred_element_type=F32
    )


def parts(a):
    high = a.astype(BF)
    return high, (a - high.astype(F32)).astype(BF)


def fine_tn(a, b):
    high_a, rest_a = parts(a)
    high_b, rest_b = parts(b)
    both = tn(jnp.concatenate([high_a, rest_a], axis=0), jnp.concatenate([high_b, high_b], axis=0))
    return both + tn(high_a, rest_b)


def grid_index(shape, dim):
    return lax.broadcasted_iota(jnp.int32, shape, dim)


def sigmoid(x):
    return 1.0 / (1.0 + jnp.exp(-x))


def softplus(x):
    return jnp.maximum(x, 0.0) + jnp.log1p(jnp.exp(-jnp.abs(x)))


def span_weights(causal, g_col, g_row):
    return jnp.where(causal, jnp.exp(jnp.where(causal, g_col - g_row, 0.0)), 0.0)


def column(row):
    size = row.shape[1]
    here = grid_index((size, size), 0) == grid_index((size, size), 1)
    return jnp.sum(jnp.where(here, row, 0.0), axis=1, keepdims=True)


def decays(decay_ref, rate_ref, bias_ref):
    rate = -jnp.exp(column(rate_ref[...]))
    logits = decay_ref[0].astype(F32) + column(bias_ref[...])
    return rate * softplus(logits), rate * sigmoid(logits)


def natural(step, core_ref, half):
    late = step >= half
    core = core_ref[0]
    return jnp.where(late, core, 1 - core) * half + jnp.where(late, step - half, step)


def store_half(early, send_ref, keep_ref, values):
    @pl.when(early)
    def _():
        for n, value in enumerate(values):
            send_ref[n] = value

    @pl.when(jnp.logical_not(early))
    def _():
        for n, value in enumerate(values):
            keep_ref[n] = value


def first_kernel(
    core_ref, k_ref, v_ref, decay_ref, beta_ref, rate_ref, bias_ref,
    kn_ref, send_ref, keep_ref, x_ref, wu_ref, col_ref, row_ref,
    g_all, column_all,
):
    step = pl.program_id(0)
    row, col = grid_index((D, D), 0), grid_index((D, D), 1)
    causal, below = row >= col, row > col
    diff = row ^ col
    heads = decay_ref.shape[1]
    count = HG * RATIO

    @pl.when(step == 0)
    def _():
        log_decay, _ = decays(decay_ref, rate_ref, bias_ref)
        upper = jnp.where(row <= col, 1.0, 0.0)
        g = jnp.dot(log_decay, upper, precision=HIGH, preferred_element_type=F32)
        g_all[...] = g
        beta = sigmoid(beta_ref[0].astype(F32))
        rest = jnp.zeros((D - 2 * heads, D), F32)
        column_all[...] = jnp.concatenate([g, beta, rest], axis=0).T

    half = pl.num_programs(0) // 2
    start = natural(step, core_ref, half) * count
    cols = pltpu.roll(column_all[...], lax.rem(D - start, D), 1)
    rows = g_all[pl.ds(pl.multiple_of(start, count), count), :]
    col_ref[0] = cols
    row_ref[...] = rows
    systems, sides, ends = [], [], []
    for j in range(HG):
        part = slice(j * D, (j + 1) * D)
        k = k_ref[0, :, part].astype(F32)
        kn = (k * lax.rsqrt(jnp.sum(k * k, axis=1, keepdims=True) + EPS)).astype(BF)
        kn_ref[:, part] = kn
        kf = kn.astype(F32)
        gram = nt(kn, kn)
        for r in range(RATIO):
            n = j * RATIO + r
            g_col, g_row = cols[:, n : n + 1], rows[n : n + 1, :]
            beta = cols[:, heads + n : heads + n + 1]
            weights = span_weights(below, g_col, g_row)
            systems.append(beta * gram * weights)
            v = v_ref[0, :, n * D : (n + 1) * D].astype(F32)
            sides.append(jnp.concatenate([kf * (beta * jnp.exp(g_col)), v * beta], axis=1))
            last = g_row[:, D - 1 :]
            ends.append((kf * jnp.exp(last - g_col), jnp.exp(last)))
    identity = jnp.where(row == col, 1.0, 0.0)
    inverse = [identity - jnp.where(diff == 1, s, 0.0) for s in systems]
    size = 2
    while size < D:
        level = (diff >= size) & (diff < 2 * size)
        low = [x.astype(BF) for x in inverse]
        inner = [nn(jnp.where(level, systems[n], 0.0), low[n]) for n in range(count)]
        inverse = [inverse[n] - nn(low[n], inner[n]) for n in range(count)]
        size *= 2
    solved = [nn(inverse[n], sides[n]) for n in range(count)]
    for n in range(count):
        x_ref[n] = inverse[n].astype(BF)
        wu_ref[n] = solved[n].astype(BF)
    closed = [fine_tn(ends[n][0], solved[n]) for n in range(count)]
    maps = [
        jnp.concatenate(
            [(identity * ends[n][1] - closed[n][:, :D]).astype(BF), closed[n][:, D:].astype(BF)], axis=1
        )
        for n in range(count)
    ]
    store_half(step < half, send_ref, keep_ref, maps)


def local_kernel(
    core_ref, q_ref, kn_ref, wu_ref, col_ref, row_ref, qn_ref, p_ref, r_ref, o_ref, mark_ref
):
    mark_ref[...] = jnp.zeros_like(mark_ref)
    causal = grid_index((D, D), 0) >= grid_index((D, D), 1)
    cols, rows = col_ref[0], row_ref[...]
    count = HG * RATIO
    for j in range(HG):
        part = slice(j * D, (j + 1) * D)
        q = q_ref[0, :, part].astype(F32)
        qn = q * lax.rsqrt(jnp.sum(q * q, axis=1, keepdims=True) + EPS) * D**-0.5
        qn_ref[:, part] = qn.astype(BF)
    scores = [
        nt(qn_ref[:, j * D : (j + 1) * D], kn_ref[:, j * D : (j + 1) * D]) for j in range(HG)
    ]
    for n in range(count):
        g_col, g_row = cols[:, n : n + 1], rows[n : n + 1, :]
        p_ref[n] = (scores[n // RATIO] * span_weights(causal, g_col, g_row)).astype(BF)
    both = [nn(p_ref[n], wu_ref[n]) for n in range(count)]
    for n in range(count):
        j = n // RATIO
        qn = qn_ref[:, j * D : (j + 1) * D].astype(F32)
        r_ref[n] = (qn * jnp.exp(cols[:, n : n + 1]) - both[n][:, :D]).astype(BF)
        o_ref[n] = both[n][:, D:]


def merge_maps(core_ref, keep_ref, got_ref, out_ref):
    first = core_ref[0] == 0
    for n in range(out_ref.shape[0]):
        keep, got = keep_ref[n].astype(F32), got_ref[n].astype(F32)
        before, after = jnp.where(first, keep, got), jnp.where(first, got, keep)
        out = nn(after[:, :D], before)
        out_ref[n, :, :D] = out[:, :D].astype(BF)
        out_ref[n, :, D:] = (out[:, D:] + after[:, D:]).astype(BF)


def place_states(core_ref, keep_ref, got_ref, start_ref, own_ref, send_ref):
    first = core_ref[0] == 0
    for n in range(start_ref.shape[0]):
        before = jnp.where(first, keep_ref[n].astype(F32), got_ref[n].astype(F32))
        start = start_ref[n].astype(F32)
        later = nn(before[:, :D], start) + before[:, D:]
        own_ref[n] = jnp.where(first, start, later).astype(BF)
        send_ref[n] = jnp.where(first, later, start).astype(BF)


def merge_sources(core_ref, keep_ref, got_ref, keep_c_ref, got_c_ref, out_ref):
    first = core_ref[0] == 0
    for n in range(out_ref.shape[0]):
        before = jnp.where(first, keep_ref[n].astype(F32), got_ref[n].astype(F32))
        keep, got = keep_c_ref[n].astype(F32), got_c_ref[n].astype(F32)
        early, late = jnp.where(first, keep, got), jnp.where(first, got, keep)
        out_ref[n] = (early + tn(before[:, :D], late)).astype(BF)


def place_grads(
    core_ref, keep_ref, got_ref, keep_c_ref, got_c_ref, end_ref, own_ref, send_ref
):
    first = core_ref[0] == 0
    for n in range(end_ref.shape[0]):
        after = jnp.where(first, got_ref[n].astype(F32), keep_ref[n].astype(F32))
        late = jnp.where(first, got_c_ref[n].astype(F32), keep_c_ref[n].astype(F32))
        end = end_ref[n].astype(F32)
        middle = late + tn(after[:, :D], end)
        own_ref[n] = jnp.where(first, middle, end).astype(BF)
        send_ref[n] = jnp.where(first, end, middle).astype(BF)


def forward_scan(ab_ref, _, s_ref):
    chunks = ab_ref.shape[0] // RATIO
    states = [jnp.zeros((D, D), F32) for _ in range(RATIO)]
    for c in range(chunks):
        for r in range(RATIO):
            n = c * RATIO + r
            high = states[r].astype(BF)
            s_ref[n] = high
            if c == chunks - 1:
                continue
            b = ab_ref[n, :, D:].astype(F32)
            if c == 0:
                states[r] = b
                continue
            rest = (states[r] - high.astype(F32)).astype(BF)
            out = nn(ab_ref[n, :, :D], jnp.concatenate([high, rest], axis=1))
            states[r] = out[:, :D] + out[:, D:] + b


def backward_scan(ab_ref, c_ref, _, e_ref):
    chunks = ab_ref.shape[0] // RATIO
    states = [jnp.zeros((D, D), F32) for _ in range(RATIO)]
    for c in reversed(range(chunks)):
        for r in range(RATIO):
            n = c * RATIO + r
            high = states[r].astype(BF)
            e_ref[n] = high
            if c == 0:
                continue
            b = c_ref[n].astype(F32)
            if c == chunks - 1:
                states[r] = b
                continue
            rest = (states[r] - high.astype(F32)).astype(BF)
            out = tn(ab_ref[n, :, :D], jnp.concatenate([high, rest], axis=1))
            states[r] = out[:, :D] + out[:, D:] + b


def norm_kernel(
    core_ref, r_ref, o_ref, got_ref, own_ref, gate_ref, dout_ref, weight_ref,
    mixed_ref, dgate_ref, dcore_ref, s_ref, send_ref, keep_ref, dnorm_ref,
):
    weight = weight_ref[...]
    early = pl.program_id(0) < pl.num_programs(0) // 2

    @pl.when(early)
    def _():
        s_ref[...] = got_ref[...]

    @pl.when(jnp.logical_not(early))
    def _():
        s_ref[...] = own_ref[...]

    @pl.when(pl.program_id(0) == 0)
    def _():
        dnorm_ref[...] = jnp.zeros_like(dnorm_ref)

    total = jnp.zeros((8, D), F32)
    carried = [nn(r_ref[n], s_ref[n]) for n in range(HG * RATIO)]
    for n in range(HG * RATIO):
        part = slice(n * D, (n + 1) * D)
        core = (carried[n] + o_ref[n]).astype(BF).astype(F32)
        gate = gate_ref[0, :, part].astype(F32)
        grad = dout_ref[0, :, part].astype(F32)
        scale = lax.rsqrt(jnp.mean(core * core, axis=1, keepdims=True) + EPS)
        sig = sigmoid(gate)
        silu = gate * sig
        y = core * scale
        yw = y * weight
        mixed_ref[0, :, part] = (yw * silu).astype(BF)
        dgate_ref[0, :, part] = (grad * yw * (sig * (1.0 + gate * (1.0 - sig)))).astype(BF)
        gs = grad * silu
        e = gs * weight
        ey = jnp.mean(e * y, axis=1, keepdims=True)
        dcore_ref[n] = ((e - y * ey) * scale).astype(BF)
        total = total + jnp.sum((gs * y).reshape(D // 8, 8, D), axis=0)
    dnorm_ref[...] += total
    sources = [tn(r_ref[n], dcore_ref[n]).astype(BF) for n in range(HG * RATIO)]
    store_half(early, send_ref, keep_ref, sources)


def score_kernel(
    core_ref, q_ref, qn_ref, kn_ref, wu_ref, x_ref, p_ref, s_ref, dcore_ref, col_ref, row_ref,
    dq_ref, n_ref, y_ref, xk_ref, gram_ref, dk_ref, drow_ref,
):
    row, col = grid_index((D, D), 0), grid_index((D, D), 1)
    causal, here = row >= col, row == col
    cols, rows = col_ref[0], row_ref[...]
    count = HG * RATIO
    taken = [nn(wu_ref[n, :, :D], s_ref[n]) for n in range(count)]
    for n in range(count):
        n_ref[n] = (wu_ref[n, :, D:].astype(F32) - taken[n]).astype(BF)
    both = [
        nt(dcore_ref[n], jnp.concatenate([n_ref[n], s_ref[n]], axis=0)) for n in range(count)
    ]
    dns = [tn(p_ref[n], dcore_ref[n]).astype(BF) for n in range(count)]
    for n in range(count):
        part = slice(n // RATIO * D, (n // RATIO + 1) * D)
        fall = jnp.exp(rows[n : n + 1, D - 1 :] - cols[:, n : n + 1])
        kd = (kn_ref[:, part].astype(F32) * fall).astype(BF)
        out = tn(x_ref[n], jnp.concatenate([dns[n], kd], axis=1))
        y_ref[n] = out[:, :D]
        xk_ref[n] = out[:, D:].astype(BF)
    for j in range(HG):
        part = slice(j * D, (j + 1) * D)
        gram_ref[j] = nt(kn_ref[:, part], kn_ref[:, part])
    dscores, dqns = [], []
    for j in range(HG):
        part = slice(j * D, (j + 1) * D)
        qf = qn_ref[:, part].astype(F32)
        dscore = jnp.zeros((D, D), F32)
        dqn = jnp.zeros((D, D), F32)
        for r in range(RATIO):
            n = j * RATIO + r
            g_col, g_row = cols[:, n : n + 1], rows[n : n + 1, :]
            dp = both[n][:, :D]
            dscore = dscore + dp * span_weights(causal, g_col, g_row)
            z = dp * p_ref[n].astype(F32)
            dqe = both[n][:, D:] * jnp.exp(g_col)
            dqn = dqn + dqe
            dg = jnp.sum(z + qf * dqe, axis=1, keepdims=True)
            drow_ref[n : n + 1, :] = jnp.sum(
                jnp.where(here, dg, 0.0) - z, axis=0, keepdims=True
            )
        dscores.append(dscore.astype(BF))
        dqns.append(dqn)
    for j in range(HG):
        part = slice(j * D, (j + 1) * D)
        dk_ref[j] = tn(dscores[j], qn_ref[:, part])
        dqn = dqns[j] + nn(dscores[j], kn_ref[:, part])
        dqn = dqn.astype(BF).astype(F32) * D**-0.5
        q = q_ref[0, :, part].astype(F32)
        inv = lax.rsqrt(jnp.sum(q * q, axis=1, keepdims=True) + EPS)
        dot = jnp.sum(q * dqn, axis=1, keepdims=True)
        dq_ref[0, :, part] = (inv * (dqn - q * (inv * inv * dot))).astype(BF)


def last_kernel(
    core_ref, v_ref, decay_ref, rate_ref, bias_ref,
    kn_ref, s_ref, got_ref, own_ref, n_ref, y_ref, xk_ref, gram_ref, dk_ref, drow_ref,
    col_ref, row_ref, dnorm_ref,
    dkn_ref, dgram_ref, dvalue_ref, ddecay_ref, dbeta_ref, sums_ref,
    dg_all, end_all, dbeta_all, e_ref,
):
    step = pl.program_id(0)
    row, col = grid_index((D, D), 0), grid_index((D, D), 1)
    below, here = row > col, row == col
    heads = decay_ref.shape[1]
    count = HG * RATIO
    cols, rows = col_ref[0], row_ref[...]
    half = pl.num_programs(0) // 2
    start = natural(step, core_ref, half) * count

    @pl.when(step < half)
    def _():
        e_ref[...] = got_ref[...]

    @pl.when(step >= half)
    def _():
        e_ref[...] = own_ref[...]

    falls = [jnp.exp(rows[n : n + 1, D - 1 :] - cols[:, n : n + 1]) for n in range(count)]
    ys = [y_ref[n] + nn(xk_ref[n], e_ref[n]) for n in range(count)]
    boths = [
        nt(ys[n], jnp.concatenate([n_ref[n], s_ref[n]], axis=0)) for n in range(count)
    ]
    dkds = [nt(n_ref[n], e_ref[n]) for n in range(count)]
    for j in range(HG):
        part = slice(j * D, (j + 1) * D)
        kf = kn_ref[:, part].astype(F32)
        dgram = jnp.zeros((D, D), F32)
        dkn = dk_ref[j]
        for r in range(RATIO):
            n = j * RATIO + r
            head = start + n
            g_col, g_row = cols[:, n : n + 1], rows[n : n + 1, :]
            beta = cols[:, heads + n : heads + n + 1]
            weights = span_weights(below, g_col, g_row)
            rise, close = jnp.exp(g_col), jnp.exp(g_row[:, D - 1 :])
            y = ys[n]
            dlower = -boths[n][:, :D] * weights
            dside = -boths[n][:, D:] * rise
            part_beta = dlower * gram_ref[j]
            dgram = dgram + dlower * beta
            dkd = dkds[n] * falls[n]
            kdkd = kf * dkd
            solved = jnp.sum(part_beta + kf * dside, axis=1, keepdims=True)
            sum_fall = jnp.sum(kdkd, axis=1, keepdims=True)
            dkn = dkn + dkd + dside * beta
            vpart = slice(n * D, (n + 1) * D)
            v = v_ref[0, :, vpart].astype(F32)
            dvalue_ref[0, :, vpart] = (y * beta).astype(BF)
            dbeta = solved + jnp.sum(v * y, axis=1, keepdims=True)
            dg = beta * solved - sum_fall
            dg_row = jnp.sum(jnp.where(here, dg, 0.0) - part_beta * beta, axis=0, keepdims=True)
            dg_all[pl.ds(head, 1), :] = dg_row + drow_ref[n : n + 1, :]
            product = s_ref[n].astype(F32) * e_ref[n].astype(F32) * close + kdkd
            end_all[pl.ds(head, 1), :] = jnp.sum(product, axis=0, keepdims=True)
            dbeta_all[pl.ds(head, 1), :] = jnp.sum(
                jnp.where(here, dbeta * (beta * (1.0 - beta)), 0.0), axis=0, keepdims=True
            )
        dgram_ref[j] = dgram.astype(BF)
        dkn_ref[j] = dkn

    @pl.when(step == pl.num_programs(0) - 1)
    def _():
        log_decay, slope = decays(decay_ref, rate_ref, bias_ref)
        lower = jnp.where(row >= col, 1.0, 0.0)
        dlog = jnp.dot(dg_all[...], lower, precision=HIGH, preferred_element_type=F32)
        dlog = dlog + jnp.sum(end_all[...], axis=1, keepdims=True)
        ddecay_ref[0] = (dlog * slope).astype(BF)
        dbeta_ref[0] = dbeta_all[...].astype(BF)
        d_rate = jnp.sum(dlog * log_decay, axis=1, keepdims=True)
        d_bias = jnp.sum(dlog * slope, axis=1, keepdims=True)
        lane = grid_index((heads, D), 1)
        which = lax.rem(grid_index((heads, D), 0), RATIO)
        own = jnp.where(lane == which, d_rate, jnp.where(lane == RATIO + which, d_bias, 0.0))
        dnorm = jnp.sum(dnorm_ref[...], axis=0, keepdims=True)
        groups = heads // RATIO
        copies = sums_ref.shape[0] // groups
        for j in range(groups):
            both = jnp.sum(own[j * RATIO : (j + 1) * RATIO, :], axis=0, keepdims=True)
            both = jnp.where(grid_index((2, D), 0) == 0, dnorm, both)
            sums_ref[pl.ds(j * copies, copies)] = jnp.broadcast_to(both[None], (copies, 2, D))


def key_kernel(core_ref, k_ref, kn_ref, dkn_ref, dgram_ref, dkey_ref, mark_ref):
    mark_ref[...] = jnp.zeros_like(mark_ref)
    for j in range(HG):
        part = slice(j * D, (j + 1) * D)
        kn = kn_ref[:, part]
        dkn = dkn_ref[j] + nn(dgram_ref[j], kn) + tn(dgram_ref[j], kn)
        dkn = dkn.astype(BF).astype(F32)
        k = k_ref[0, :, part].astype(F32)
        inv = lax.rsqrt(jnp.sum(k * k, axis=1, keepdims=True) + EPS)
        dot = jnp.sum(k * dkn, axis=1, keepdims=True)
        dkey_ref[0, :, part] = (inv * (dkn - k * (inv * inv * dot))).astype(BF)


def sum_kernel(parts_ref, _, rate_ref, bias_ref, norm_ref):
    total = jnp.sum(parts_ref[...], axis=0)
    rate_ref[...] = total[1:2, :RATIO]
    bias_ref[...] = total[1:2, RATIO : 2 * RATIO]
    norm_ref[...] = total[0:1, :]


def params(room):
    return pltpu.CompilerParams(
        dimension_semantics=("arbitrary",), vmem_limit_bytes=room * 1024 * 1024
    )


def cost(products, moved):
    return pl.CostEstimate(flops=products * 2 * D**3 * 8, bytes_accessed=moved, transcendentals=0)


def shards(query, key, value, gate_in, decay_in, beta_in, a_log, dt_bias, norm_weight, d_out):
    hk = query.shape[2] // D
    hv = value.shape[2] // D
    steps = hk // HG
    half = steps // 2
    count = HG * RATIO
    owned = hv // 2
    rate, bias, weight = a_log[None], dt_bias[None], norm_weight[None]
    decay_rows = jnp.transpose(decay_in, (0, 2, 1))
    beta_rows = jnp.transpose(beta_in, (0, 2, 1))
    ranks = lax.axis_size("seq")
    copies = lax.axis_size("dp")
    core = lax.rem(lax.axis_index("seq"), 2).astype(jnp.int32)[None]
    shape = jax.ShapeDtypeStruct

    def tokens(width):
        return pl.BlockSpec((1, D, width), lambda i, c: (0, 0, natural(i, c, half)))

    def flat(width):
        return pl.BlockSpec((D, width), lambda i, c: (0, i))

    def lead(*dims):
        return pl.BlockSpec(dims, lambda i, c: (i,) + (0,) * (len(dims) - 1))

    def sent(*dims):
        return pl.BlockSpec(dims, lambda i, c: (jnp.minimum(i, half - 1),) + (0,) * (len(dims) - 1))

    def kept(*dims):
        return pl.BlockSpec(dims, lambda i, c: (jnp.maximum(i - half, 0),) + (0,) * (len(dims) - 1))

    def whole(*dims):
        return pl.BlockSpec(dims, lambda i, c: (0,) * len(dims))

    def call(kernel, grid, ins, outs, out_shape, spent, name, scratch=(), room=56):
        return pl.pallas_call(
            kernel,
            grid_spec=pltpu.PrefetchScalarGridSpec(
                num_scalar_prefetch=1, grid=(grid,), in_specs=ins, out_specs=outs,
                scratch_shapes=list(scratch),
            ),
            out_shape=out_shape,
            compiler_params=params(room),
            cost_estimate=spent,
            name=name,
        )

    def to_owners(array):
        groups = [list(range(c, ranks, 2)) for c in range(2)]
        return lax.all_to_all(
            array, "seq", split_axis=0, concat_axis=0, axis_index_groups=groups, tiled=True
        )

    def to_sibling(array):
        return lax.ppermute(array, "seq", [(i, i ^ 1) for i in range(ranks)])

    small, scalars = whole(1, hv, D), whole(1, hv)
    columns, rows_of = lead(1, D, D), lead(count, D)
    square, wide = lead(count, D, D), lead(count, D, 2 * D)
    half_square, half_wide = shape((owned, D, D), BF), shape((owned, D, 2 * D), BF)
    merges = owned // count
    vmem, anywhere = pl.BlockSpec(memory_space=pltpu.VMEM), pl.BlockSpec(memory_space=pl.ANY)

    kn, ab_send, ab, x, wu, cols, rows = call(
        first_kernel,
        steps,
        [tokens(HG * D), tokens(count * D), small, small, scalars, scalars],
        [
            flat(HG * D), sent(count, D, 2 * D), kept(count, D, 2 * D), square, wide,
            columns, rows_of,
        ],
        [
            shape((D, hk * D), BF), half_wide, half_wide,
            shape((hv, D, D), BF), shape((hv, D, 2 * D), BF), shape((steps, D, D), F32),
            shape((hv, D), F32),
        ],
        cost(18 * hv, 8 << 20),
        "block_solve",
        [pltpu.VMEM((hv, D), F32), pltpu.VMEM((D, D), F32)],
    )(core, key, value, decay_rows, beta_rows, rate, bias)

    ab_got = to_sibling(ab_send)
    merged = call(
        merge_maps, merges, [wide, wide], wide, half_wide, cost(owned, 3 << 20), "merge_maps", room=24
    )(core, ab, ab_got)
    ab_owned = to_owners(merged)

    qn, p, r, o, mark = call(
        local_kernel,
        steps,
        [tokens(HG * D), flat(HG * D), wide, columns, rows_of],
        [flat(HG * D), square, square, square, whole(8, D)],
        [
            shape((D, hk * D), BF), shape((hv, D, D), BF), shape((hv, D, D), BF),
            shape((hv, D, D), F32), shape((8, D), F32),
        ],
        cost(3 * hv, 8 << 20),
        "block_scores",
    )(core, query, kn, wu, cols, rows)

    s_owned = pl.pallas_call(
        forward_scan,
        in_specs=[vmem, anywhere],
        out_shape=half_square,
        compiler_params=pltpu.CompilerParams(vmem_limit_bytes=16 * 1024 * 1024),
        cost_estimate=cost(hv, 2 << 20),
        name="state_scan",
    )(ab_owned, mark)
    s_start = to_owners(s_owned)
    s_own, s_send = call(
        place_states, merges, [wide, wide, square], [square, square], [half_square, half_square],
        cost(owned, 3 << 20), "place_states", room=24,
    )(core, ab, ab_got, s_start)
    s_got = to_sibling(s_send)

    mixed, d_gate, d_core, s, c_send, c, d_norm = call(
        norm_kernel,
        steps,
        [
            square, square, sent(count, D, D), kept(count, D, D), tokens(count * D),
            tokens(count * D), whole(1, D),
        ],
        [
            tokens(count * D), tokens(count * D), square, square, sent(count, D, D),
            kept(count, D, D), whole(8, D),
        ],
        [
            shape((1, D, hv * D), BF), shape((1, D, hv * D), BF), shape((hv, D, D), BF),
            shape((hv, D, D), BF), half_square, half_square, shape((8, D), F32),
        ],
        cost(2 * hv, 10 << 20),
        "gated_norm", room=48,
    )(core, r, o, s_got, s_own, gate_in, d_out, weight)

    c_got = to_sibling(c_send)
    c_merged = call(
        merge_sources, merges, [wide, wide, square, square], square, half_square,
        cost(owned, 3 << 20), "merge_sources", room=24,
    )(core, ab, ab_got, c, c_got)
    c_owned = to_owners(c_merged)

    d_query, newest, y, xk, gram, dk, drow = call(
        score_kernel,
        steps,
        [
            tokens(HG * D), flat(HG * D), flat(HG * D), wide, square, square, square, square,
            columns, rows_of,
        ],
        [
            tokens(HG * D), square, square, square, lead(HG, D, D), lead(HG, D, D), rows_of,
        ],
        [
            shape((1, D, hk * D), BF), shape((hv, D, D), BF), shape((hv, D, D), F32),
            shape((hv, D, D), BF), shape((hk, D, D), F32), shape((hk, D, D), F32),
            shape((hv, D), F32),
        ],
        cost(6 * hv, 12 << 20),
        "score_grads",
    )(core, query, qn, kn, wu, x, p, s, d_core, cols, rows)

    e_owned = pl.pallas_call(
        backward_scan,
        in_specs=[vmem, vmem, anywhere],
        out_shape=half_square,
        compiler_params=pltpu.CompilerParams(vmem_limit_bytes=16 * 1024 * 1024),
        cost_estimate=cost(hv, 2 << 20),
        name="state_grad_scan",
    )(ab_owned, c_owned, drow)
    e_end = to_owners(e_owned)
    e_own, e_send = call(
        place_grads, merges, [wide, wide, square, square, square], [square, square],
        [half_square, half_square], cost(owned, 4 << 20), "place_grads", room=24,
    )(core, ab, ab_got, c, c_got, e_end)
    e_got = to_sibling(e_send)

    dkn, dgram, d_value, d_decay, d_beta, sums = call(
        last_kernel,
        steps,
        [
            tokens(count * D), small, scalars, scalars, flat(HG * D), square,
            sent(count, D, D), kept(count, D, D), square, square, square, lead(HG, D, D),
            lead(HG, D, D), rows_of, columns, rows_of, whole(8, D),
        ],
        [
            lead(HG, D, D), lead(HG, D, D), tokens(count * D), small, small,
            whole(ranks * copies, 2, D),
        ],
        [
            shape((hk, D, D), F32), shape((hk, D, D), BF), shape((1, D, hv * D), BF), shape((1, hv, D), BF),
            shape((1, hv, D), BF), shape((ranks * copies, 2, D), F32),
        ],
        cost(8 * hv, 14 << 20),
        "solve_grads", room=48,
        scratch=[pltpu.VMEM((hv, D), F32)] * 3 + [pltpu.VMEM((count, D, D), BF)],
    )(
        core, value, decay_rows, rate, bias, kn, s, e_got, e_own, newest, y, xk, gram, dk, drow,
        cols, rows, d_norm,
    )

    sums = lax.all_to_all(sums, ("seq", "dp"), split_axis=0, concat_axis=0, tiled=True)
    d_key, done = call(
        key_kernel,
        steps,
        [tokens(HG * D), flat(HG * D), lead(HG, D, D), lead(HG, D, D)],
        [tokens(HG * D), whole(8, D)],
        [shape((1, D, hk * D), BF), shape((8, D), F32)],
        cost(hv, 3 << 20),
        "key_grads", room=48,
    )(core, key, kn, dkn, dgram)
    d_rate, d_bias, d_weight = pl.pallas_call(
        sum_kernel,
        in_specs=[vmem, anywhere],
        out_shape=[shape((1, RATIO), F32), shape((1, RATIO), F32), shape((1, D), F32)],
        compiler_params=pltpu.CompilerParams(vmem_limit_bytes=16 * 1024 * 1024),
        name="end_sums",
    )(sums, done)
    return (
        mixed, d_query, d_key, d_value, d_gate,
        jnp.transpose(d_decay, (0, 2, 1)), jnp.transpose(d_beta, (0, 2, 1)),
        d_rate[0], d_bias[0], d_weight[0],
    )


def solution(mesh):
    row = P("dp", "seq", None)
    return jax.shard_map(
        shards,
        mesh=mesh,
        in_specs=(row, row, row, row, row, row, P(), P(), P(), row),
        out_specs=(row, row, row, row, row, row, row, P("seq"), P("seq"), P()),
        check_vma=False,
    )
```
